256 devices in a mesh: row: 8 (over z_hi, x), col: 32 (over y, z_lo, core).
Axes of the slice: x: 4, y: 4, z: 8 (z_hi: 2, z_lo: 4; z = z_hi * 4 + z_lo), core: 2. Of those that a mesh axis runs over, the one named last changes fastest.
Arguments:
- inputs: bfloat16 [512, 12288], P('col', 'row'), may hold values from -6 to 6
- up_weight: bfloat16 [12288, 24576], P('row', 'col'), may hold values from -0.0546875 to 0.0546875
- down_weight: bfloat16 [24576, 12288], P('col', 'row'), may hold values from -0.0390625 to 0.0390625
- out_grad: bfloat16 [512, 12288], P('col', 'row'), may hold values from -6 to 6
Outputs:
- outputs: bfloat16 [512, 12288], P('col', 'row')
- in_grad: bfloat16 [512, 12288], P('col', 'row')
- up_grad: bfloat16 [12288, 24576], P('row', 'col')
- down_grad: bfloat16 [24576, 12288], P('col', 'row')
The draws below stay inside these ranges and needn't reach their ends.
All inputs are finite; a program needn't handle non-finite values.
Results may differ from the reference program's by a relative error of at most 0.005.
Values may be sent and summed in bfloat16 or wider, within the bound.
A program may use at most 64 MiB of HBM per device.

```python
import jax
import jax.numpy as jnp
from jax import lax

D = 12288
FF = 24576
TOKENS = 512


def level_of(key, extent, pieces, least, high):
    def one(position, parts):
        draws = jax.random.uniform(jax.random.fold_in(jax.random.fold_in(key, 6), position), (parts,), jnp.float32, least / len(pieces), high / len(pieces))
        return jnp.repeat(jnp.exp(draws), extent[position] // parts).reshape((-1,) + (1,) * (len(extent) - position - 1))

    loudness = one(*pieces[0])
    for cut in pieces[1:]:
        loudness = loudness * one(*cut)
    return loudness


def scatter_about(own_key, shape, scale, most, split=(), kind=jnp.bfloat16):
    gain = level_of(own_key, shape, split, -0.22, 0.18) if split else 1.0
    result = jax.random.normal(own_key, shape, jnp.float32) * scale * gain
    return jnp.minimum(jnp.maximum(result, -most), most).astype(kind)


def setup_inputs(seed: int = 0) -> dict:
    keys = jax.random.split(jax.random.key(seed), 5)
    return {
        "inputs": scatter_about(keys[0], (TOKENS, D), 1.0, 6.0, ((0, 32), (1, 8))),
        "up_weight": scatter_about(keys[1], (D, FF), D ** -0.5, 0.0546875, ((0, 8), (1, 32))),
        "down_weight": scatter_about(keys[2], (FF, D), FF ** -0.5, 0.0390625, ((0, 32), (1, 8))),
        "out_grad": scatter_about(keys[3], (TOKENS, D), 1.0, 6.0, ((0, 32), (1, 8))),
    }


gelu_coef = 0.7978845608
cube_coef = 0.044715


def activate(hidden):
    tangent = jnp.tanh(gelu_coef * (hidden + cube_coef * hidden * hidden * hidden))
    return 0.5 * hidden * (1.0 + tangent)


def slope(hidden):
    tangent = jnp.tanh(gelu_coef * (hidden + cube_coef * hidden * hidden * hidden))
    inner = gelu_coef * (1.0 + 3.0 * cube_coef * hidden * hidden)
    return 0.5 * (1.0 + tangent) + 0.5 * hidden * (1.0 - tangent * tangent) * inner


def reference(inputs, up_weight, down_weight, out_grad):
    first = (((0,), (0,)), ((), ()))
    second = (((1,), (1,)), ((), ()))
    hidden = jnp.dot(inputs, up_weight, preferred_element_type=jnp.float32)
    active = activate(hidden).astype(jnp.bfloat16)
    outputs = jnp.dot(active, down_weight, preferred_element_type=jnp.float32).astype(jnp.bfloat16)
    down_grad = lax.dot_general(active, out_grad, first, preferred_element_type=jnp.float32).astype(jnp.bfloat16)
    act_grad = lax.dot_general(out_grad, down_weight, second, preferred_element_type=jnp.float32)
    hid_grad = (act_grad * slope(hidden)).astype(jnp.bfloat16)
    up_grad = lax.dot_general(inputs, hid_grad, first, preferred_element_type=jnp.float32).astype(jnp.bfloat16)
    in_grad = lax.dot_general(hid_grad, up_weight, second, preferred_element_type=jnp.float32).astype(jnp.bfloat16)
    return (outputs, in_grad, up_grad, down_grad)
```

```python
import functools

import jax
import jax.numpy as jnp
from jax import lax
from jax.experimental import pallas as pl
from jax.experimental.pallas import tpu as pltpu
from jax.sharding import PartitionSpec as P

MESH = pl.DeviceIdType.MESH
F32, BF16 = jnp.float32, jnp.bfloat16

gelu_coef = 0.7978845608
cube_coef = 0.044715

ORDER = (
    ("first", 0, 0), ("first", 1, 0), ("weights", 0, 0),
    ("relay", 0, 1), ("relay", 0, 2), ("relay", 0, 3),
    ("up", 0, 0),
    ("relay", 1, 1), ("relay", 1, 2),
    ("pass", 0, 1), ("relay", 1, 3), ("pass", 0, 3), ("pass", 0, 2),
    ("up", 0, 1), ("rowsum", 0, 0), ("up", 1, 0), ("up", 0, 3), ("up", 0, 2),
    ("act", 0, 0), ("rowsum", 0, 1),
    ("pass", 1, 1), ("pass", 1, 3), ("pass", 1, 2),
    ("up", 1, 1), ("spread", 0, 0), ("rowsum", 1, 0), ("up", 1, 3), ("act", 0, 1), ("up", 1, 2),
    ("rowsum", 0, 3), ("act", 1, 0), ("rowsum", 0, 2), ("spread", 0, 1),
    ("act", 0, 3), ("rowsum", 1, 1), ("spread", 1, 0), ("act", 0, 2),
    ("down", 0, 0), ("spread", 0, 3), ("act", 1, 1), ("rowsum", 1, 3), ("spread", 0, 2),
    ("pair", 0, 0), ("rowsum", 1, 2), ("spread", 1, 1), ("act", 1, 3),
    ("down", 0, 1), ("act", 1, 2), ("down", 1, 0), ("spread", 1, 3), ("pair", 0, 1),
    ("spread", 1, 2), ("down", 0, 3), ("pair", 1, 0), ("down", 0, 2), ("pair", 0, 3),
    ("pair", 0, 2), ("down", 1, 1), ("down", 1, 3), ("pair", 1, 1), ("down", 1, 2), ("pair", 1, 3),
    ("colsum", 0, 0), ("pair", 1, 2), ("grad", 0, 0), ("colsum", 1, 0), ("grad", 1, 0),
    ("finish", 0, 0), ("finish", 1, 0),
)


def kernel(
    x_ref, g_ref, wu_hbm, wd_hbm,
    out_ref, in_grad_ref, up_grad_hbm, down_grad_hbm,
    wu, wd, wut, wdt, gather, part, send_x, recv_x, own_x, send_z, recv_z, slopes, act,
    prod, recv_c, send_y, recv_y, own_y, send_f, recv_f, own_f, up_grad, down_grad,
    wsem, osem, sent, gz, gy, gs, gs0, rx, rz, az, ax, rc, ry, rf,
):
    row, col = lax.axis_index("row"), lax.axis_index("col")
    x, h = lax.rem(row, 4), row // 4
    y, zl, k = col // 8, lax.rem(col // 2, 4), lax.rem(col, 2)

    def at(dx=0, dh=0, dy=0, dz=0, dk=0):
        r = lax.rem(h + dh, 2) * 4 + lax.rem(x + dx, 4)
        c = lax.rem(y + dy, 4) * 8 + lax.rem(zl + dz, 4) * 2 + lax.rem(k + dk, 2)
        return (r, c)

    loads = [
        pltpu.make_async_copy(wu_hbm, wu, wsem.at[0]),
        pltpu.make_async_copy(wd_hbm, wd, wsem.at[1]),
    ]
    for load in loads:
        load.start()

    barrier = pltpu.get_barrier_semaphore()
    partners = [dict(dk=1), dict(dh=1)]
    for j in (1, 2, 3):
        partners += [dict(dx=j), dict(dy=j), dict(dz=j)]
    for partner in partners:
        pl.semaphore_signal(barrier, inc=1, device_id=at(**partner), device_id_type=MESH)
    pl.semaphore_wait(barrier, len(partners))

    sends = []

    def send(src, dst, sem, **where):
        copy = pltpu.make_async_remote_copy(
            src_ref=src, dst_ref=dst, send_sem=sent.at[len(sends)], recv_sem=sem,
            device_id=at(**where), device_id_type=MESH,
        )
        copy.start()
        sends.append(copy)

    def arrive(dst, sem):
        pltpu.make_async_remote_copy(
            src_ref=dst, dst_ref=dst, send_sem=sent.at[0], recv_sem=sem,
            device_id=at(dk=1), device_id_type=MESH,
        ).wait_recv()

    def rows(start, size):
        return pl.ds(pl.multiple_of(start, 16), size)

    def place(core, z):
        return rows(core * 64 + z * 16, 16)

    sources = (x_ref, g_ref)

    def first(c, _):
        src = sources[c]
        for j in (1, 2, 3):
            send(src, gather.at[c, 0, place(k, zl)], gz.at[c, j - 1], dz=j)
        for d in (1, 3, 2):
            send(src, gather.at[c, 4 - d, place(k, zl)], gy.at[c, 4 - d, 0], dy=d)
        send(src, gather.at[c, 0, place(k, zl)], gs0.at[c, 0], dk=1)
        gather[c, 0, place(k, zl)] = src[...]

    def weights(c, _):
        for load in loads:
            load.wait()
        for j in range(3):
            wut[j * 256:(j + 1) * 256, :] = wu[:, j * 256:(j + 1) * 256].T
        for j in range(6):
            wdt[j * 256:(j + 1) * 256, :] = wd[:, j * 256:(j + 1) * 256].T

    def relay(c, j):
        piece = gather.at[c, 0, place(k, lax.rem(zl + 4 - j, 4))]
        arrive(piece, gz.at[c, j - 1])
        for d in (1, 3, 2):
            send(piece, gather.at[c, 4 - d, place(k, lax.rem(zl + 4 - j, 4))], gy.at[c, 4 - d, j], dy=d)
        send(piece, piece, gs0.at[c, j], dk=1)

    def pass_on(c, d):
        for j in range(4):
            arrive(gather.at[c, d, place(k, lax.rem(zl + 4 - j, 4))], gy.at[c, d, j])
        half = gather.at[c, d, rows(k * 64, 64)]
        send(half, half, gs.at[c, d], dk=1)

    def up(c, d):
        if d == 0:
            for j in range(4):
                arrive(gather.at[c, 0, place(1 - k, lax.rem(zl + 4 - j, 4))], gs0.at[c, j])
        else:
            arrive(gather.at[c, d, rows((1 - k) * 64, 64)], gs.at[c, d])
        weight = (wu, wdt)[c]
        part[c, d] = jnp.dot(gather[c, d], weight[...], preferred_element_type=F32)
        send_x[c, d] = part[c, d].astype(BF16)
        for j in (1, 3, 2):
            send(send_x.at[c, d, rows(lax.rem(x + j, 4) * 32, 32)], recv_x.at[c, d, j - 1], rx.at[c, d, j - 1], dx=j)

    def rowsum(c, d):
        for j in (1, 2, 3):
            arrive(recv_x.at[c, d, j - 1], rx.at[c, d, j - 1])
        total = part[c, d, rows(x * 32, 32)]
        for j in (1, 2, 3):
            total = total + recv_x[c, d, j - 1].astype(F32)
        own_x[c, d] = total
        send_z[c, d] = own_x[c, d, rows((1 - h) * 16, 16)].astype(BF16)
        send(send_z.at[c, d], recv_z.at[c, d], rz.at[c, d], dh=1)

    def mine(half):
        return rows(x * 32 + half * 16, 16)

    def act_step(c, d):
        arrive(recv_z.at[c, d], rz.at[c, d])
        total = own_x[c, d, rows(h * 16, 16)] + recv_z[c, d].astype(F32)
        if c == 0:
            tangent = jnp.tanh(gelu_coef * (total + cube_coef * total * total * total))
            inner = gelu_coef * (1.0 + 3.0 * cube_coef * total * total)
            slopes[d] = 0.5 * (1.0 + tangent) + 0.5 * total * (1.0 - tangent * tangent) * inner
            result = 0.5 * total * (1.0 + tangent)
        else:
            result = total * slopes[d]
        act[c, d, mine(h)] = result.astype(BF16)
        send(act.at[c, d, mine(h)], act.at[c, d, mine(h)], az.at[c, d], dh=1)

    def spread(c, d):
        arrive(act.at[c, d, mine(1 - h)], az.at[c, d])
        for j in (1, 3, 2):
            send(act.at[c, d, rows(x * 32, 32)], act.at[c, d, rows(x * 32, 32)], ax.at[c, d, j - 1], dx=j)

    def down(c, d):
        for j in (1, 2, 3):
            arrive(act.at[c, d, rows(lax.rem(x + 4 - j, 4) * 32, 32)], ax.at[c, d, j - 1])
        weight = (wd, wut)[c]
        prod[c, d] = jnp.dot(act[c, d], weight[...], preferred_element_type=F32)
        send(prod.at[c, d, rows((1 - k) * 64, 64)], recv_c.at[c, d], rc.at[c, d], dk=1)

    def pair(c, d):
        arrive(recv_c.at[c, d], rc.at[c, d])
        total = prod[c, d, rows(k * 64, 64)] + recv_c[c, d]
        if d == 0:
            own_y[c] = total
        else:
            send_y[c, d - 1] = total.astype(BF16)
            send(send_y.at[c, d - 1], recv_y.at[c, d - 1], ry.at[c, d - 1], dy=d)

    def colsum(c, _):
        for d in (1, 2, 3):
            arrive(recv_y.at[c, d - 1], ry.at[c, d - 1])
        total = own_y[c]
        for d in (1, 2, 3):
            total = total + recv_y[c, d - 1].astype(F32)
        own_y[c] = total
        send_f[c] = total.astype(BF16)
        for j in (1, 3, 2):
            send(send_f.at[c, rows(lax.rem(zl + j, 4) * 16, 16)], recv_f.at[c, j - 1], rf.at[c, j - 1], dz=j)

    results = (out_ref, in_grad_ref)

    def finish(c, _):
        for j in (1, 2, 3):
            arrive(recv_f.at[c, j - 1], rf.at[c, j - 1])
        total = own_y[c, rows(zl * 16, 16)]
        for j in (1, 2, 3):
            total = total + recv_f[c, j - 1].astype(F32)
        results[c][...] = total.astype(BF16)

    stores = []

    def grad(c, _):
        left, right = ((act, gather), (gather, act))[c]
        target, home = ((down_grad, down_grad_hbm), (up_grad, up_grad_hbm))[c]
        a = left[0, :].reshape(512, left.shape[3])
        width = right.shape[3]
        for n in range(0, width, 256):
            b = right[1, :, :, n:n + 256].reshape(512, 256)
            target[:, n:n + 256] = lax.dot_general(
                a, b, (((0,), (0,)), ((), ())), preferred_element_type=F32
            ).astype(BF16)
        store = pltpu.make_async_copy(target, home, osem.at[c])
        store.start()
        stores.append(store)

    steps = dict(
        first=first, weights=weights, relay=relay, up=up, rowsum=rowsum, act=act_step, spread=spread,
        down=down, pair=pair, colsum=colsum, finish=finish, grad=grad,
    )
    steps["pass"] = pass_on
    for name, c, d in ORDER:
        steps[name](c, d)
    for store in stores:
        store.wait()
    for copy in sends:
        copy.wait_send()


def shards(inputs, up_weight, down_weight, out_grad):
    t, dm = inputs.shape
    ff = up_weight.shape[1]
    vmem = pl.BlockSpec(memory_space=pltpu.VMEM)
    anywhere = pl.BlockSpec(memory_space=pl.ANY)
    dma = pltpu.SemaphoreType.DMA
    outputs, in_grad, up_grad, down_grad = pl.pallas_call(
        kernel,
        out_shape=(
            jax.ShapeDtypeStruct((t, dm), BF16),
            jax.ShapeDtypeStruct((t, dm), BF16),
            jax.ShapeDtypeStruct((dm, ff), BF16),
            jax.ShapeDtypeStruct((ff, dm), BF16),
        ),
        in_specs=[vmem, vmem, anywhere, anywhere],
        out_specs=(vmem, vmem, anywhere, anywhere),
        scratch_shapes=[
            pltpu.VMEM((dm, ff), BF16),
            pltpu.VMEM((ff, dm), BF16),
            pltpu.VMEM((ff, dm), BF16),
            pltpu.VMEM((dm, ff), BF16),
            pltpu.VMEM((2, 4, 128, dm), BF16),
            pltpu.VMEM((2, 4, 128, ff), F32),
            pltpu.VMEM((2, 4, 128, ff), BF16),
            pltpu.VMEM((2, 4, 3, 32, ff), BF16),
            pltpu.VMEM((2, 4, 32, ff), F32),
            pltpu.VMEM((2, 4, 16, ff), BF16),
            pltpu.VMEM((2, 4, 16, ff), BF16),
            pltpu.VMEM((4, 16, ff), F32),
            pltpu.VMEM((2, 4, 128, ff), BF16),
            pltpu.VMEM((2, 4, 128, dm), F32),
            pltpu.VMEM((2, 4, 64, dm), F32),
            pltpu.VMEM((2, 3, 64, dm), BF16),
            pltpu.VMEM((2, 3, 64, dm), BF16),
            pltpu.VMEM((2, 64, dm), F32),
            pltpu.VMEM((2, 64, dm), BF16),
            pltpu.VMEM((2, 3, 16, dm), BF16),
            pltpu.VMEM((8, 128), F32),
            pltpu.VMEM((dm, ff), BF16),
            pltpu.VMEM((ff, dm), BF16),
            dma((2,)),
            dma((2,)),
            dma((160,)),
            dma((2, 3)),
            dma((2, 4, 4)),
            dma((2, 4)),
            dma((2, 4)),
            dma((2, 4, 3)),
            dma((2, 4)),
            dma((2, 4)),
            dma((2, 4, 3)),
            dma((2, 4)),
            dma((2, 3)),
            dma((2, 3)),
        ],
        compiler_params=pltpu.CompilerParams(
            collective_id=0, has_side_effects=True, vmem_limit_bytes=58 << 20
        ),
        name="block",
    )(inputs, out_grad, up_weight, down_weight)
    return outputs, in_grad, up_grad, down_grad


def solution(mesh):
    in_specs = (P("col", "row"), P("row", "col"), P("col", "row"), P("col", "row"))
    out_specs = (P("col", "row"), P("col", "row"), P("row", "col"), P("col", "row"))
    return jax.shard_map(shards, mesh=mesh, in_specs=in_specs, out_specs=out_specs, check_vma=False)
```

```python
import functools

import jax
import jax.numpy as jnp
from jax import lax
from jax.experimental import pallas as pl
from jax.experimental.pallas import tpu as pltpu
from jax.sharding import PartitionSpec as P

MESH = pl.DeviceIdType.MESH
F32, BF16 = jnp.float32, jnp.bfloat16

gelu_coef = 0.7978845608
cube_coef = 0.044715

ORDER = (
    ("first", 0, 0), ("first", 1, 0), ("weights", 0, 0), ("relay", 0, 1), ("relay", 0, 2), ("relay", 0, 3),
    ("relay", 1, 1), ("up", 0, 0), ("pass", 0, 1), ("pass", 0, 3), ("relay", 1, 2), ("relay", 1, 3), ("up", 0, 1),
    ("up", 0, 3), ("rowsum", 0, 0), ("pass", 0, 2), ("up", 0, 2), ("pass", 1, 1), ("pass", 1, 3), ("rowsum", 0, 1),
    ("up", 1, 1), ("rowsum", 0, 3), ("up", 1, 3), ("pass", 1, 2), ("rowsum", 0, 2), ("up", 1, 2), ("act", 0, 1),
    ("rowsum", 1, 1), ("act", 0, 3), ("rowsum", 1, 3), ("up", 1, 0), ("act", 0, 2), ("rowsum", 1, 2), ("down", 0, 1),
    ("act", 1, 1), ("down", 0, 3), ("pair", 0, 1), ("act", 1, 2), ("rowsum", 1, 0), ("act", 0, 0), ("act", 1, 3),
    ("pair", 0, 3), ("down", 0, 2), ("pair", 0, 2), ("down", 1, 1), ("act", 1, 0), ("down", 1, 2), ("pair", 1, 2),
    ("down", 0, 0), ("grad", 0, 0), ("down", 1, 3), ("pair", 1, 1), ("pair", 0, 0), ("colsum", 0, 0),
    ("colsum", 0, 1), ("colsum", 0, 3), ("colsum", 0, 2), ("pair", 1, 3), ("down", 1, 0), ("grad", 1, 0),
    ("pair", 1, 0), ("colsum", 1, 0), ("colsum", 1, 1), ("finish", 0, 0), ("colsum", 1, 2), ("colsum", 1, 3),
    ("finish", 1, 0),
)


def kernel(
    x_ref, g_ref, wu_hbm, wd_hbm,
    out_ref, in_grad_ref, up_grad, down_grad,
    wu, wd, wut, wdt, gather, part, send_x, recv_x, own_x, send_z, recv_z, slopes, act,
    prod, recv_c, send_y, recv_y, own_y, send_f, recv_f, own_f,
    wsem, sent, gz, gy, gf, gs, gs0, rx, rz, ax, rc, ry, rf,
):
    row, col = lax.axis_index("row"), lax.axis_index("col")
    x, h = lax.rem(row, 4), row // 4
    y, zl, k = col // 8, lax.rem(col // 2, 4), lax.rem(col, 2)

    def at(dx=0, dh=0, dy=0, dz=0, dk=0):
        r = lax.rem(h + dh, 2) * 4 + lax.rem(x + dx, 4)
        c = lax.rem(y + dy, 4) * 8 + lax.rem(zl + dz, 4) * 2 + lax.rem(k + dk, 2)
        return (r, c)

    loads = [
        pltpu.make_async_copy(wu_hbm, wu, wsem.at[0]),
        pltpu.make_async_copy(wd_hbm, wd, wsem.at[1]),
    ]
    for load in loads:
        load.start()

    barrier = pltpu.get_barrier_semaphore()
    partners = [dict(dk=1), dict(dh=1)]
    for j in (1, 2, 3):
        partners += [dict(dx=j), dict(dy=j), dict(dz=j)]
    for partner in partners:
        pl.semaphore_signal(barrier, inc=1, device_id=at(**partner), device_id_type=MESH)
    pl.semaphore_wait(barrier, len(partners))

    sends = []

    def send(src, dst, sem, **where):
        copy = pltpu.make_async_remote_copy(
            src_ref=src, dst_ref=dst, send_sem=sent.at[len(sends)], recv_sem=sem,
            device_id=at(**where), device_id_type=MESH,
        )
        copy.start()
        sends.append(copy)

    def arrive(dst, sem):
        pltpu.make_async_remote_copy(
            src_ref=dst, dst_ref=dst, send_sem=sent.at[0], recv_sem=sem,
            device_id=at(dk=1), device_id_type=MESH,
        ).wait_recv()

    def rows(start, size):
        return pl.ds(pl.multiple_of(start, 16), size)

    def place(core, z):
        return rows(core * 64 + z * 16, 16)

    sources = (x_ref, g_ref)

    def first(c, _):
        src = sources[c]
        for j in (1, 2, 3):
            send(src, gather.at[c, 0, place(k, zl)], gz.at[c, j - 1], dz=j)
        for d in (1, 3):
            send(src, gather.at[c, 4 - d, place(k, zl)], gy.at[c, 4 - d, 0], dy=d)
        send(src, gather.at[c, 0, place(k, zl)], gs0.at[c, 0], dk=1)
        gather[c, 0, place(k, zl)] = src[...]

    def weights(c, _):
        for load in loads:
            load.wait()
        for j in range(3):
            wut[j * 256:(j + 1) * 256, :] = wu[:, j * 256:(j + 1) * 256].T
        for j in range(6):
            wdt[j * 256:(j + 1) * 256, :] = wd[:, j * 256:(j + 1) * 256].T

    def relay(c, j):
        piece = gather.at[c, 0, place(k, lax.rem(zl + 4 - j, 4))]
        arrive(piece, gz.at[c, j - 1])
        for d in (1, 3):
            send(piece, gather.at[c, 4 - d, place(k, lax.rem(zl + 4 - j, 4))], gy.at[c, 4 - d, j], dy=d)
        send(piece, piece, gs0.at[c, j], dk=1)

    def pass_on(c, d):
        if d == 2:
            for side in (0, 1):
                arrive(gather.at[c, 2, rows(k * 64 + side * 32, 32)], gf.at[c, side])
        else:
            for j in range(4):
                arrive(gather.at[c, d, place(k, lax.rem(zl + 4 - j, 4))], gy.at[c, d, j])
            side = 0 if d == 3 else 1
            piece = rows(k * 64 + side * 32, 32)
            send(gather.at[c, d, piece], gather.at[c, 2, piece], gf.at[c, side], dy=4 - d)
        half = gather.at[c, d, rows(k * 64, 64)]
        send(half, half, gs.at[c, d], dk=1)

    def up(c, d):
        if d == 0:
            for j in range(4):
                arrive(gather.at[c, 0, place(1 - k, lax.rem(zl + 4 - j, 4))], gs0.at[c, j])
        else:
            arrive(gather.at[c, d, rows((1 - k) * 64, 64)], gs.at[c, d])
        weight = (wu, wdt)[c]
        part[c, d] = jnp.dot(gather[c, d], weight[...], preferred_element_type=F32)
        send_x[c, d] = part[c, d].astype(BF16)
        for j in (1, 3, 2):
            send(send_x.at[c, d, rows(lax.rem(x + j, 4) * 32, 32)], recv_x.at[c, d, j - 1], rx.at[c, d, j - 1], dx=j)

    def rowsum(c, d):
        for j in (1, 2, 3):
            arrive(recv_x.at[c, d, j - 1], rx.at[c, d, j - 1])
        total = part[c, d, rows(x * 32, 32)]
        for j in (1, 2, 3):
            total = total + recv_x[c, d, j - 1].astype(F32)
        own_x[c, d] = total
        send_z[c, d] = total.astype(BF16)
        send(send_z.at[c, d], recv_z.at[c, d], rz.at[c, d], dh=1)

    def act_step(c, d):
        arrive(recv_z.at[c, d], rz.at[c, d])
        total = own_x[c, d] + recv_z[c, d].astype(F32)
        if c == 0:
            tangent = jnp.tanh(gelu_coef * (total + cube_coef * total * total * total))
            inner = gelu_coef * (1.0 + 3.0 * cube_coef * total * total)
            slopes[d] = 0.5 * (1.0 + tangent) + 0.5 * total * (1.0 - tangent * tangent) * inner
            result = 0.5 * total * (1.0 + tangent)
        else:
            result = total * slopes[d]
        mine = rows(x * 32, 32)
        act[c, d, mine] = result.astype(BF16)
        for j in (1, 3, 2):
            send(act.at[c, d, mine], act.at[c, d, mine], ax.at[c, d, j - 1], dx=j)

    def down(c, d):
        for j in (1, 2, 3):
            arrive(act.at[c, d, rows(lax.rem(x + 4 - j, 4) * 32, 32)], ax.at[c, d, j - 1])
        weight = (wd, wut)[c]
        prod[c, d] = jnp.dot(act[c, d], weight[...], preferred_element_type=F32)
        send(prod.at[c, d, rows((1 - k) * 64, 64)], recv_c.at[c, d], rc.at[c, d], dk=1)

    def pair(c, d):
        arrive(recv_c.at[c, d], rc.at[c, d])
        total = prod[c, d, rows(k * 64, 64)] + recv_c[c, d]
        if d == 0:
            own_y[c] = total
        else:
            send_y[c, d - 1] = total.astype(BF16)
            for j in (1, 2, 3, 0):
                piece = rows(lax.rem(zl + j, 4) * 16, 16)
                send(send_y.at[c, d - 1, piece], recv_y.at[c, d - 1, piece], ry.at[c, d - 1, j], dy=d)

    def colsum(c, p):
        j = (p + 1) % 4
        piece = rows(lax.rem(zl + j, 4) * 16, 16)
        for d in (1, 2, 3):
            arrive(recv_y.at[c, d - 1, piece], ry.at[c, d - 1, j])
        total = own_y[c, piece]
        for d in (1, 2, 3):
            total = total + recv_y[c, d - 1, piece].astype(F32)
        if j == 0:
            own_f[c] = total
        else:
            send_f[c, piece] = total.astype(BF16)
            send(send_f.at[c, piece], recv_f.at[c, j - 1], rf.at[c, j - 1], dz=j)

    results = (out_ref, in_grad_ref)

    def finish(c, _):
        for j in (1, 2, 3):
            arrive(recv_f.at[c, j - 1], rf.at[c, j - 1])
        total = own_f[c]
        for j in (1, 2, 3):
            total = total + recv_f[c, j - 1].astype(F32)
        results[c][...] = total.astype(BF16)

    def grad(c, _):
        left, right = ((act, gather), (gather, act))[c]
        target = (down_grad, up_grad)[c]
        a = left[0, :].reshape(512, left.shape[3])
        width = right.shape[3]
        for n in range(0, width, 256):
            b = right[1, :, :, n:n + 256].reshape(512, 256)
            target[:, n:n + 256] = lax.dot_general(
                a, b, (((0,), (0,)), ((), ())), preferred_element_type=F32
            ).astype(BF16)

    steps = dict(
        first=first, weights=weights, relay=relay, up=up, rowsum=rowsum, act=act_step,
        down=down, pair=pair, colsum=colsum, finish=finish, grad=grad,
    )
    steps["pass"] = pass_on
    for name, c, d in ORDER:
        steps[name](c, d)
    for copy in sends:
        copy.wait_send()


def store(*refs):
    sems = refs[8]
    copies = [pltpu.make_async_copy(refs[i], refs[4 + i], sems.at[i]) for i in range(4)]
    for copy in copies:
        copy.start()
    for copy in copies:
        copy.wait()


def shards(inputs, up_weight, down_weight, out_grad):
    t, dm = inputs.shape
    ff = up_weight.shape[1]
    vmem = pl.BlockSpec(memory_space=pltpu.VMEM)
    anywhere = pl.BlockSpec(memory_space=pl.ANY)
    dma = pltpu.SemaphoreType.DMA
    results = pl.pallas_call(
        kernel,
        out_shape=(
            pltpu.VMEM((t, dm), BF16),
            pltpu.VMEM((t, dm), BF16),
            pltpu.VMEM((dm, ff), BF16),
            pltpu.VMEM((ff, dm), BF16),
        ),
        in_specs=[vmem, vmem, anywhere, anywhere],
        out_specs=(vmem,) * 4,
        scratch_shapes=[
            pltpu.VMEM((dm, ff), BF16),
            pltpu.VMEM((ff, dm), BF16),
            pltpu.VMEM((ff, dm), BF16),
            pltpu.VMEM((dm, ff), BF16),
            pltpu.VMEM((2, 4, 128, dm), BF16),
            pltpu.VMEM((2, 4, 128, ff), F32),
            pltpu.VMEM((2, 4, 128, ff), BF16),
            pltpu.VMEM((2, 4, 3, 32, ff), BF16),
            pltpu.VMEM((2, 4, 32, ff), F32),
            pltpu.VMEM((2, 4, 32, ff), BF16),
            pltpu.VMEM((2, 4, 32, ff), BF16),
            pltpu.VMEM((4, 32, ff), F32),
            pltpu.VMEM((2, 4, 128, ff), BF16),
            pltpu.VMEM((2, 4, 128, dm), F32),
            pltpu.VMEM((2, 4, 64, dm), F32),
            pltpu.VMEM((2, 3, 64, dm), BF16),
            pltpu.VMEM((2, 3, 64, dm), BF16),
            pltpu.VMEM((2, 64, dm), F32),
            pltpu.VMEM((2, 64, dm), BF16),
            pltpu.VMEM((2, 3, 16, dm), BF16),
            pltpu.VMEM((2, 16, dm), F32),
            dma((2,)),
            dma((160,)),
            dma((2, 3)),
            dma((2, 4, 4)),
            dma((2, 2)),
            dma((2, 4)),
            dma((2, 4)),
            dma((2, 4, 3)),
            dma((2, 4)),
            dma((2, 4, 3)),
            dma((2, 4)),
            dma((2, 3, 4)),
            dma((2, 3)),
        ],
        compiler_params=pltpu.CompilerParams(
            collective_id=0, has_side_effects=True, vmem_limit_bytes=58 << 20
        ),
        name="block",
    )(inputs, out_grad, up_weight, down_weight)
    return pl.pallas_call(
        store,
        out_shape=tuple(jax.ShapeDtypeStruct(r.shape, r.dtype) for r in results),
        in_specs=[vmem] * 4,
        out_specs=(anywhere,) * 4,
        scratch_shapes=[dma((4,))],
        compiler_params=pltpu.CompilerParams(vmem_limit_bytes=1 << 20),
        name="store",
    )(*results)


def solution(mesh):
    in_specs = (P("col", "row"), P("row", "col"), P("col", "row"), P("col", "row"))
    out_specs = (P("col", "row"), P("col", "row"), P("row", "col"), P("col", "row"))
    return jax.shard_map(shards, mesh=mesh, in_specs=in_specs, out_specs=out_specs, check_vma=False)
```

```python
import functools

import jax
import jax.numpy as jnp
from jax import lax
from jax.experimental import pallas as pl
from jax.experimental.pallas import tpu as pltpu
from jax.sharding import PartitionSpec as P

MESH = pl.DeviceIdType.MESH
F32, BF16 = jnp.float32, jnp.bfloat16

gelu_coef = 0.7978845608
cube_coef = 0.044715

ORDER = (
    ("first", 0, 0), ("weights", 0, 0), ("relay", 0, 1), ("relay", 0, 2), ("relay", 0, 3), ("first", 1, 0),
    ("up", 0, 0), ("pass", 0, 1), ("pass", 0, 3), ("relay", 1, 1), ("relay", 1, 2), ("relay", 1, 3), ("up", 0, 1),
    ("up", 0, 3), ("rowsum", 0, 0), ("pass", 0, 2), ("up", 0, 2), ("pass", 1, 1), ("pass", 1, 3), ("rowsum", 0, 1),
    ("up", 1, 1), ("rowsum", 0, 3), ("up", 1, 3), ("pass", 1, 2), ("rowsum", 0, 2), ("up", 1, 2), ("act", 0, 1),
    ("rowsum", 1, 1), ("act", 0, 3), ("rowsum", 1, 3), ("up", 1, 0), ("act", 0, 2), ("rowsum", 1, 2), ("down", 0, 1),
    ("act", 1, 1), ("down", 0, 3), ("pair", 0, 1), ("act", 1, 2), ("rowsum", 1, 0), ("act", 0, 0), ("act", 1, 3),
    ("pair", 0, 3), ("down", 0, 2), ("pair", 0, 2), ("down", 1, 1), ("act", 1, 0), ("down", 1, 2), ("pair", 1, 2),
    ("down", 0, 0), ("grad", 0, 0), ("down", 1, 3), ("pair", 1, 1), ("pair", 0, 0), ("colsum", 0, 0),
    ("colsum", 0, 1), ("colsum", 0, 3), ("colsum", 0, 2), ("pair", 1, 3), ("down", 1, 0), ("grad", 1, 0),
    ("pair", 1, 0), ("colsum", 1, 0), ("colsum", 1, 1), ("finish", 0, 0), ("colsum", 1, 2), ("colsum", 1, 3),
    ("finish", 1, 0),
)


def kernel(
    x_ref, g_ref, wu_hbm, wd_hbm,
    out_ref, in_grad_ref, up_grad, down_grad,
    wu, wd, wut, wdt, gather, part, send_x, recv_x, own_x, send_z, recv_z, slopes, act,
    prod, recv_c, send_y, recv_y, own_y, send_f, recv_f, own_f,
    wsem, sent, gz, gy, gf, gs, gs0, rx, rz, ax, rc, ry, rf,
):
    row, col = lax.axis_index("row"), lax.axis_index("col")
    x, h = lax.rem(row, 4), row // 4
    y, zl, k = col // 8, lax.rem(col // 2, 4), lax.rem(col, 2)

    def at(dx=0, dh=0, dy=0, dz=0, dk=0):
        r = lax.rem(h + dh, 2) * 4 + lax.rem(x + dx, 4)
        c = lax.rem(y + dy, 4) * 8 + lax.rem(zl + dz, 4) * 2 + lax.rem(k + dk, 2)
        return (r, c)

    loads = [
        pltpu.make_async_copy(wu_hbm, wu, wsem.at[0]),
        pltpu.make_async_copy(wd_hbm, wd, wsem.at[1]),
    ]
    for load in loads:
        load.start()

    barrier = pltpu.get_barrier_semaphore()
    partners = [dict(dk=1), dict(dh=1)]
    for j in (1, 2, 3):
        partners += [dict(dx=j), dict(dy=j), dict(dz=j)]
    for partner in partners:
        pl.semaphore_signal(barrier, inc=1, device_id=at(**partner), device_id_type=MESH)
    pl.semaphore_wait(barrier, len(partners))

    sends = []

    def send(src, dst, sem, **where):
        copy = pltpu.make_async_remote_copy(
            src_ref=src, dst_ref=dst, send_sem=sent.at[len(sends)], recv_sem=sem,
            device_id=at(**where), device_id_type=MESH,
        )
        copy.start()
        sends.append(copy)

    def arrive(dst, sem):
        pltpu.make_async_remote_copy(
            src_ref=dst, dst_ref=dst, send_sem=sent.at[0], recv_sem=sem,
            device_id=at(dk=1), device_id_type=MESH,
        ).wait_recv()

    def rows(start, size):
        return pl.ds(pl.multiple_of(start, 16), size)

    def place(core, z):
        return rows(core * 64 + z * 16, 16)

    sources = (x_ref, g_ref)

    def first(c, _):
        src = sources[c]
        for j in (1, 2, 3):
            send(src, gather.at[c, 0, place(k, zl)], gz.at[c, j - 1], dz=j)
        for d in (1, 3):
            send(src, gather.at[c, 4 - d, place(k, zl)], gy.at[c, 4 - d, 0], dy=d)
        send(src, gather.at[c, 0, place(k, zl)], gs0.at[c, 0], dk=1)
        gather[c, 0, place(k, zl)] = src[...]

    def weights(c, _):
        for load in loads:
            load.wait()
        for j in range(3):
            wut[j * 256:(j + 1) * 256, :] = wu[:, j * 256:(j + 1) * 256].T
        for j in range(6):
            wdt[j * 256:(j + 1) * 256, :] = wd[:, j * 256:(j + 1) * 256].T

    def relay(c, j):
        piece = gather.at[c, 0, place(k, lax.rem(zl + 4 - j, 4))]
        arrive(piece, gz.at[c, j - 1])
        for d in (1, 3):
            send(piece, gather.at[c, 4 - d, place(k, lax.rem(zl + 4 - j, 4))], gy.at[c, 4 - d, j], dy=d)
        send(piece, piece, gs0.at[c, j], dk=1)

    def pass_on(c, d):
        if d == 2:
            for side in (0, 1):
                arrive(gather.at[c, 2, rows(k * 64 + side * 32, 32)], gf.at[c, side])
        else:
            for j in range(4):
                arrive(gather.at[c, d, place(k, lax.rem(zl + 4 - j, 4))], gy.at[c, d, j])
            side = 0 if d == 3 else 1
            piece = rows(k * 64 + side * 32, 32)
            send(gather.at[c, d, piece], gather.at[c, 2, piece], gf.at[c, side], dy=4 - d)
        half = gather.at[c, d, rows(k * 64, 64)]
        send(half, half, gs.at[c, d], dk=1)

    def up(c, d):
        if d == 0:
            for j in range(4):
                arrive(gather.at[c, 0, place(1 - k, lax.rem(zl + 4 - j, 4))], gs0.at[c, j])
        else:
            arrive(gather.at[c, d, rows((1 - k) * 64, 64)], gs.at[c, d])
        weight = (wu, wdt)[c]
        part[c, d] = jnp.dot(gather[c, d], weight[...], preferred_element_type=F32)
        send_x[c, d] = part[c, d].astype(BF16)
        for j in (2, 1, 3):
            send(send_x.at[c, d, rows(lax.rem(x + j, 4) * 32, 32)], recv_x.at[c, d, j - 1], rx.at[c, d, j - 1], dx=j)

    def rowsum(c, d):
        for j in (1, 2, 3):
            arrive(recv_x.at[c, d, j - 1], rx.at[c, d, j - 1])
        total = part[c, d, rows(x * 32, 32)]
        for j in (1, 2, 3):
            total = total + recv_x[c, d, j - 1].astype(F32)
        own_x[c, d] = total
        send_z[c, d] = total.astype(BF16)
        send(send_z.at[c, d], recv_z.at[c, d], rz.at[c, d], dh=1)

    def act_step(c, d):
        arrive(recv_z.at[c, d], rz.at[c, d])
        total = own_x[c, d] + recv_z[c, d].astype(F32)
        if c == 0:
            tangent = jnp.tanh(gelu_coef * (total + cube_coef * total * total * total))
            inner = gelu_coef * (1.0 + 3.0 * cube_coef * total * total)
            slopes[d] = 0.5 * (1.0 + tangent) + 0.5 * total * (1.0 - tangent * tangent) * inner
            result = 0.5 * total * (1.0 + tangent)
        else:
            result = total * slopes[d]
        mine = rows(x * 32, 32)
        act[c, d, mine] = result.astype(BF16)
        for j in (2, 1, 3):
            send(act.at[c, d, mine], act.at[c, d, mine], ax.at[c, d, j - 1], dx=j)

    def down(c, d):
        for j in (1, 2, 3):
            arrive(act.at[c, d, rows(lax.rem(x + 4 - j, 4) * 32, 32)], ax.at[c, d, j - 1])
        weight = (wd, wut)[c]
        prod[c, d] = jnp.dot(act[c, d], weight[...], preferred_element_type=F32)
        send(prod.at[c, d, rows((1 - k) * 64, 64)], recv_c.at[c, d], rc.at[c, d], dk=1)

    def pair(c, d):
        arrive(recv_c.at[c, d], rc.at[c, d])
        total = prod[c, d, rows(k * 64, 64)] + recv_c[c, d]
        if d == 0:
            own_y[c] = total
        else:
            send_y[c, d - 1] = total.astype(BF16)
            for j in (1, 2, 3, 0):
                piece = rows(lax.rem(zl + j, 4) * 16, 16)
                send(send_y.at[c, d - 1, piece], recv_y.at[c, d - 1, piece], ry.at[c, d - 1, j], dy=d)

    def colsum(c, p):
        j = (p + 1) % 4
        piece = rows(lax.rem(zl + j, 4) * 16, 16)
        for d in (1, 2, 3):
            arrive(recv_y.at[c, d - 1, piece], ry.at[c, d - 1, j])
        total = own_y[c, piece]
        for d in (1, 2, 3):
            total = total + recv_y[c, d - 1, piece].astype(F32)
        if j == 0:
            own_f[c] = total
        else:
            send_f[c, piece] = total.astype(BF16)
            send(send_f.at[c, piece], recv_f.at[c, j - 1], rf.at[c, j - 1], dz=j)

    results = (out_ref, in_grad_ref)

    def finish(c, _):
        for j in (1, 2, 3):
            arrive(recv_f.at[c, j - 1], rf.at[c, j - 1])
        total = own_f[c]
        for j in (1, 2, 3):
            total = total + recv_f[c, j - 1].astype(F32)
        results[c][...] = total.astype(BF16)

    def grad(c, _):
        left, right = ((act, gather), (gather, act))[c]
        target = (down_grad, up_grad)[c]
        a = left[0, :].reshape(512, left.shape[3])
        width = right.shape[3]
        for n in range(0, width, 256):
            b = right[1, :, :, n:n + 256].reshape(512, 256)
            target[:, n:n + 256] = lax.dot_general(
                a, b, (((0,), (0,)), ((), ())), preferred_element_type=F32
            ).astype(BF16)

    steps = dict(
        first=first, weights=weights, relay=relay, up=up, rowsum=rowsum, act=act_step,
        down=down, pair=pair, colsum=colsum, finish=finish, grad=grad,
    )
    steps["pass"] = pass_on
    for name, c, d in ORDER:
        steps[name](c, d)
    for copy in sends:
        copy.wait_send()


def store(*refs):
    sems = refs[8]
    copies = [pltpu.make_async_copy(refs[i], refs[4 + i], sems.at[i]) for i in range(4)]
    for copy in copies:
        copy.start()
    for copy in copies:
        copy.wait()


def shards(inputs, up_weight, down_weight, out_grad):
    t, dm = inputs.shape
    ff = up_weight.shape[1]
    vmem = pl.BlockSpec(memory_space=pltpu.VMEM)
    anywhere = pl.BlockSpec(memory_space=pl.ANY)
    dma = pltpu.SemaphoreType.DMA
    results = pl.pallas_call(
        kernel,
        out_shape=(
            pltpu.VMEM((t, dm), BF16),
            pltpu.VMEM((t, dm), BF16),
            pltpu.VMEM((dm, ff), BF16),
            pltpu.VMEM((ff, dm), BF16),
        ),
        in_specs=[vmem, vmem, anywhere, anywhere],
        out_specs=(vmem,) * 4,
        scratch_shapes=[
            pltpu.VMEM((dm, ff), BF16),
            pltpu.VMEM((ff, dm), BF16),
            pltpu.VMEM((ff, dm), BF16),
            pltpu.VMEM((dm, ff), BF16),
            pltpu.VMEM((2, 4, 128, dm), BF16),
            pltpu.VMEM((2, 4, 128, ff), F32),
            pltpu.VMEM((2, 4, 128, ff), BF16),
            pltpu.VMEM((2, 4, 3, 32, ff), BF16),
            pltpu.VMEM((2, 4, 32, ff), F32),
            pltpu.VMEM((2, 4, 32, ff), BF16),
            pltpu.VMEM((2, 4, 32, ff), BF16),
            pltpu.VMEM((4, 32, ff), F32),
            pltpu.VMEM((2, 4, 128, ff), BF16),
            pltpu.VMEM((2, 4, 128, dm), F32),
            pltpu.VMEM((2, 4, 64, dm), F32),
            pltpu.VMEM((2, 3, 64, dm), BF16),
            pltpu.VMEM((2, 3, 64, dm), BF16),
            pltpu.VMEM((2, 64, dm), F32),
            pltpu.VMEM((2, 64, dm), BF16),
            pltpu.VMEM((2, 3, 16, dm), BF16),
            pltpu.VMEM((2, 16, dm), F32),
            dma((2,)),
            dma((160,)),
            dma((2, 3)),
            dma((2, 4, 4)),
            dma((2, 2)),
            dma((2, 4)),
            dma((2, 4)),
            dma((2, 4, 3)),
            dma((2, 4)),
            dma((2, 4, 3)),
            dma((2, 4)),
            dma((2, 3, 4)),
            dma((2, 3)),
        ],
        compiler_params=pltpu.CompilerParams(
            collective_id=0, has_side_effects=True, vmem_limit_bytes=58 << 20
        ),
        name="block",
    )(inputs, out_grad, up_weight, down_weight)
    return pl.pallas_call(
        store,
        out_shape=tuple(jax.ShapeDtypeStruct(r.shape, r.dtype) for r in results),
        in_specs=[vmem] * 4,
        out_specs=(anywhere,) * 4,
        scratch_shapes=[dma((4,))],
        compiler_params=pltpu.CompilerParams(vmem_limit_bytes=1 << 20),
        name="store",
    )(*results)


def solution(mesh):
    in_specs = (P("col", "row"), P("row", "col"), P("col", "row"), P("col", "row"))
    out_specs = (P("col", "row"), P("col", "row"), P("row", "col"), P("col", "row"))
    return jax.shard_map(shards, mesh=mesh, in_specs=in_specs, out_specs=out_specs, check_vma=False)
```

```python
import functools

import jax
import jax.numpy as jnp
from jax import lax
from jax.experimental import pallas as pl
from jax.experimental.pallas import tpu as pltpu
from jax.sharding import PartitionSpec as P

MESH = pl.DeviceIdType.MESH
F32, BF16 = jnp.float32, jnp.bfloat16

gelu_coef = 0.7978845608
cube_coef = 0.044715

ORDER = (
    ("first", 0, 0), ("weights", 0, 0), ("relay", 0, 1), ("relay", 0, 2), ("relay", 0, 3), ("first", 1, 0),
    ("up", 0, 0), ("pass", 0, 1), ("pass", 0, 3), ("relay", 1, 1), ("relay", 1, 2), ("relay", 1, 3), ("up", 0, 1),
    ("up", 0, 3), ("rowsum", 0, 0), ("pass", 0, 2), ("up", 0, 2), ("pass", 1, 1), ("pass", 1, 3), ("rowsum", 0, 1),
    ("up", 1, 1), ("rowsum", 0, 3), ("up", 1, 3), ("pass", 1, 2), ("rowsum", 0, 2), ("up", 1, 2), ("act", 0, 1),
    ("rowsum", 1, 1), ("act", 0, 3), ("rowsum", 1, 3), ("up", 1, 0), ("act", 0, 2), ("rowsum", 1, 2), ("down", 0, 1),
    ("act", 1, 1), ("down", 0, 3), ("pair", 0, 1), ("act", 1, 2), ("rowsum", 1, 0), ("act", 1, 3), ("act", 0, 0),
    ("pair", 0, 3), ("down", 0, 2), ("pair", 0, 2), ("down", 1, 1), ("act", 1, 0), ("down", 1, 2), ("pair", 1, 2),
    ("down", 0, 0), ("grad", 0, 0), ("down", 1, 3), ("pair", 1, 1), ("pair", 0, 0), ("colsum", 0, 0),
    ("colsum", 0, 1), ("colsum", 0, 3), ("colsum", 0, 2), ("pair", 1, 3), ("down", 1, 0), ("grad", 1, 0),
    ("pair", 1, 0), ("colsum", 1, 0), ("colsum", 1, 1), ("finish", 0, 0), ("colsum", 1, 2), ("colsum", 1, 3),
    ("finish", 1, 0),
)


def kernel(
    x_ref, g_ref, wu_hbm, wd_hbm,
    out_ref, in_grad_ref, up_grad, down_grad,
    wu, wd, wut, wdt, gather, part, send_x, recv_x, own_x, send_z, recv_z, slopes, act,
    prod, recv_c, send_y, recv_y, own_y, send_f, recv_f, own_f,
    wsem, sent, gz, gy, gf, gs, gs0, rx, rz, ax, rc, ry, rf,
):
    row, col = lax.axis_index("row"), lax.axis_index("col")
    x, h = lax.rem(row, 4), row // 4
    y, zl, k = col // 8, lax.rem(col // 2, 4), lax.rem(col, 2)

    def at(dx=0, dh=0, dy=0, dz=0, dk=0):
        r = lax.rem(h + dh, 2) * 4 + lax.rem(x + dx, 4)
        c = lax.rem(y + dy, 4) * 8 + lax.rem(zl + dz, 4) * 2 + lax.rem(k + dk, 2)
        return (r, c)

    loads = [
        pltpu.make_async_copy(wu_hbm, wu, wsem.at[0]),
        pltpu.make_async_copy(wd_hbm, wd, wsem.at[1]),
    ]
    for load in loads:
        load.start()

    barrier = pltpu.get_barrier_semaphore()
    partners = [dict(dk=1), dict(dh=1)]
    for j in (1, 2, 3):
        partners += [dict(dx=j), dict(dy=j), dict(dz=j)]
    for partner in partners:
        pl.semaphore_signal(barrier, inc=1, device_id=at(**partner), device_id_type=MESH)
    pl.semaphore_wait(barrier, len(partners))

    sends = []

    def send(src, dst, sem, **where):
        copy = pltpu.make_async_remote_copy(
            src_ref=src, dst_ref=dst, send_sem=sent.at[len(sends)], recv_sem=sem,
            device_id=at(**where), device_id_type=MESH,
        )
        copy.start()
        sends.append(copy)

    def arrive(dst, sem):
        pltpu.make_async_remote_copy(
            src_ref=dst, dst_ref=dst, send_sem=sent.at[0], recv_sem=sem,
            device_id=at(dk=1), device_id_type=MESH,
        ).wait_recv()

    def rows(start, size):
        return pl.ds(pl.multiple_of(start, 16), size)

    def place(core, z):
        return rows(core * 64 + z * 16, 16)

    sources = (x_ref, g_ref)

    def first(c, _):
        src = sources[c]
        for j in (1, 2, 3):
            send(src, gather.at[c, 0, place(k, zl)], gz.at[c, j - 1], dz=j)
        for d in (1, 3):
            send(src, gather.at[c, 4 - d, place(k, zl)], gy.at[c, 4 - d, 0], dy=d)
        send(src, gather.at[c, 0, place(k, zl)], gs0.at[c, 0], dk=1)
        gather[c, 0, place(k, zl)] = src[...]

    def weights(c, _):
        for load in loads:
            load.wait()
        for j in range(3):
            wut[j * 256:(j + 1) * 256, :] = wu[:, j * 256:(j + 1) * 256].T
        for j in range(6):
            wdt[j * 256:(j + 1) * 256, :] = wd[:, j * 256:(j + 1) * 256].T

    def relay(c, j):
        piece = gather.at[c, 0, place(k, lax.rem(zl + 4 - j, 4))]
        arrive(piece, gz.at[c, j - 1])
        for d in (1, 3):
            send(piece, gather.at[c, 4 - d, place(k, lax.rem(zl + 4 - j, 4))], gy.at[c, 4 - d, j], dy=d)
        send(piece, piece, gs0.at[c, j], dk=1)

    def pass_on(c, d):
        if d == 2:
            for side in (0, 1):
                arrive(gather.at[c, 2, rows(k * 64 + side * 32, 32)], gf.at[c, side])
        else:
            for j in range(4):
                arrive(gather.at[c, d, place(k, lax.rem(zl + 4 - j, 4))], gy.at[c, d, j])
            side = 0 if d == 3 else 1
            piece = rows(k * 64 + side * 32, 32)
            send(gather.at[c, d, piece], gather.at[c, 2, piece], gf.at[c, side], dy=4 - d)
        half = gather.at[c, d, rows(k * 64, 64)]
        send(half, half, gs.at[c, d], dk=1)

    def up(c, d):
        if d == 0:
            for j in range(4):
                arrive(gather.at[c, 0, place(1 - k, lax.rem(zl + 4 - j, 4))], gs0.at[c, j])
        else:
            arrive(gather.at[c, d, rows((1 - k) * 64, 64)], gs.at[c, d])
        weight = (wu, wdt)[c]
        part[c, d] = jnp.dot(gather[c, d], weight[...], preferred_element_type=F32)
        send_x[c, d] = part[c, d].astype(BF16)
        for j in (2, 1, 3):
            send(send_x.at[c, d, rows(lax.rem(x + j, 4) * 32, 32)], recv_x.at[c, d, j - 1], rx.at[c, d, j - 1], dx=j)

    def rowsum(c, d):
        for j in (1, 2, 3):
            arrive(recv_x.at[c, d, j - 1], rx.at[c, d, j - 1])
        total = part[c, d, rows(x * 32, 32)]
        for j in (1, 2, 3):
            total = total + recv_x[c, d, j - 1].astype(F32)
        own_x[c, d] = total
        send_z[c, d] = total.astype(BF16)
        send(send_z.at[c, d], recv_z.at[c, d], rz.at[c, d], dh=1)

    def act_step(c, d):
        arrive(recv_z.at[c, d], rz.at[c, d])
        total = own_x[c, d] + recv_z[c, d].astype(F32)
        if c == 0:
            tangent = jnp.tanh(gelu_coef * (total + cube_coef * total * total * total))
            inner = gelu_coef * (1.0 + 3.0 * cube_coef * total * total)
            slopes[d] = 0.5 * (1.0 + tangent) + 0.5 * total * (1.0 - tangent * tangent) * inner
            result = 0.5 * total * (1.0 + tangent)
        else:
            result = total * slopes[d]
        mine = rows(x * 32, 32)
        act[c, d, mine] = result.astype(BF16)
        for j in (2, 1, 3):
            send(act.at[c, d, mine], act.at[c, d, mine], ax.at[c, d, j - 1], dx=j)

    def down(c, d):
        for j in (1, 2, 3):
            arrive(act.at[c, d, rows(lax.rem(x + 4 - j, 4) * 32, 32)], ax.at[c, d, j - 1])
        weight = (wd, wut)[c]
        prod[c, d] = jnp.dot(act[c, d], weight[...], preferred_element_type=F32)
        send(prod.at[c, d, rows((1 - k) * 64, 64)], recv_c.at[c, d], rc.at[c, d], dk=1)

    def pair(c, d):
        arrive(recv_c.at[c, d], rc.at[c, d])
        total = prod[c, d, rows(k * 64, 64)] + recv_c[c, d]
        if d == 0:
            own_y[c] = total
        else:
            send_y[c, d - 1] = total.astype(BF16)
            for j in (1, 2, 3, 0):
                piece = rows(lax.rem(zl + j, 4) * 16, 16)
                send(send_y.at[c, d - 1, piece], recv_y.at[c, d - 1, piece], ry.at[c, d - 1, j], dy=d)

    def colsum(c, p):
        j = (p + 1) % 4
        piece = rows(lax.rem(zl + j, 4) * 16, 16)
        for d in (1, 2, 3):
            arrive(recv_y.at[c, d - 1, piece], ry.at[c, d - 1, j])
        total = own_y[c, piece]
        for d in (1, 2, 3):
            total = total + recv_y[c, d - 1, piece].astype(F32)
        if j == 0:
            own_f[c] = total
        else:
            send_f[c, piece] = total.astype(BF16)
            send(send_f.at[c, piece], recv_f.at[c, j - 1], rf.at[c, j - 1], dz=j)

    results = (out_ref, in_grad_ref)

    def finish(c, _):
        for j in (1, 2, 3):
            arrive(recv_f.at[c, j - 1], rf.at[c, j - 1])
        total = own_f[c]
        for j in (1, 2, 3):
            total = total + recv_f[c, j - 1].astype(F32)
        results[c][...] = total.astype(BF16)

    def grad(c, _):
        left, right = ((act, gather), (gather, act))[c]
        target = (down_grad, up_grad)[c]
        a = left[0, :].reshape(512, left.shape[3])
        width = right.shape[3]
        for n in range(0, width, 256):
            b = right[1, :, :, n:n + 256].reshape(512, 256)
            target[:, n:n + 256] = lax.dot_general(
                a, b, (((0,), (0,)), ((), ())), preferred_element_type=F32
            ).astype(BF16)

    steps = dict(
        first=first, weights=weights, relay=relay, up=up, rowsum=rowsum, act=act_step,
        down=down, pair=pair, colsum=colsum, finish=finish, grad=grad,
    )
    steps["pass"] = pass_on
    for name, c, d in ORDER:
        steps[name](c, d)
    for copy in sends:
        copy.wait_send()


def store(*refs):
    sems = refs[8]
    copies = [pltpu.make_async_copy(refs[i], refs[4 + i], sems.at[i]) for i in range(4)]
    for copy in copies:
        copy.start()
    for copy in copies:
        copy.wait()


def shards(inputs, up_weight, down_weight, out_grad):
    t, dm = inputs.shape
    ff = up_weight.shape[1]
    vmem = pl.BlockSpec(memory_space=pltpu.VMEM)
    anywhere = pl.BlockSpec(memory_space=pl.ANY)
    dma = pltpu.SemaphoreType.DMA
    results = pl.pallas_call(
        kernel,
        out_shape=(
            pltpu.VMEM((t, dm), BF16),
            pltpu.VMEM((t, dm), BF16),
            pltpu.VMEM((dm, ff), BF16),
            pltpu.VMEM((ff, dm), BF16),
        ),
        in_specs=[vmem, vmem, anywhere, anywhere],
        out_specs=(vmem,) * 4,
        scratch_shapes=[
            pltpu.VMEM((dm, ff), BF16),
            pltpu.VMEM((ff, dm), BF16),
            pltpu.VMEM((ff, dm), BF16),
            pltpu.VMEM((dm, ff), BF16),
            pltpu.VMEM((2, 4, 128, dm), BF16),
            pltpu.VMEM((2, 4, 128, ff), F32),
            pltpu.VMEM((2, 4, 128, ff), BF16),
            pltpu.VMEM((2, 4, 3, 32, ff), BF16),
            pltpu.VMEM((2, 4, 32, ff), F32),
            pltpu.VMEM((2, 4, 32, ff), BF16),
            pltpu.VMEM((2, 4, 32, ff), BF16),
            pltpu.VMEM((4, 32, ff), F32),
            pltpu.VMEM((2, 4, 128, ff), BF16),
            pltpu.VMEM((2, 4, 128, dm), F32),
            pltpu.VMEM((2, 4, 64, dm), F32),
            pltpu.VMEM((2, 3, 64, dm), BF16),
            pltpu.VMEM((2, 3, 64, dm), BF16),
            pltpu.VMEM((2, 64, dm), F32),
            pltpu.VMEM((2, 64, dm), BF16),
            pltpu.VMEM((2, 3, 16, dm), BF16),
            pltpu.VMEM((2, 16, dm), F32),
            dma((2,)),
            dma((160,)),
            dma((2, 3)),
            dma((2, 4, 4)),
            dma((2, 2)),
            dma((2, 4)),
            dma((2, 4)),
            dma((2, 4, 3)),
            dma((2, 4)),
            dma((2, 4, 3)),
            dma((2, 4)),
            dma((2, 3, 4)),
            dma((2, 3)),
        ],
        compiler_params=pltpu.CompilerParams(
            collective_id=0, has_side_effects=True, vmem_limit_bytes=58 << 20
        ),
        name="block",
    )(inputs, out_grad, up_weight, down_weight)
    return pl.pallas_call(
        store,
        out_shape=tuple(jax.ShapeDtypeStruct(r.shape, r.dtype) for r in results),
        in_specs=[vmem] * 4,
        out_specs=(anywhere,) * 4,
        scratch_shapes=[dma((4,))],
        compiler_params=pltpu.CompilerParams(vmem_limit_bytes=1 << 20),
        name="store",
    )(*results)


def solution(mesh):
    in_specs = (P("col", "row"), P("row", "col"), P("col", "row"), P("col", "row"))
    out_specs = (P("col", "row"), P("col", "row"), P("row", "col"), P("col", "row"))
    return jax.shard_map(shards, mesh=mesh, in_specs=in_specs, out_specs=out_specs, check_vma=False)
```
